128 devices in a mesh: shell: 8 (over y_hi, x), order: 16 (over y_lo, z, core).
Axes of the slice: x: 4, y: 4 (y_hi: 2, y_lo: 2; y = y_hi * 2 + y_lo), z: 4, core: 2. Of those that a mesh axis runs over, the one named last changes fastest.
Arguments:
- velocity: bfloat16 [2, 2, 128, 128, 1024], P(None, None, 'order', 'shell'), may hold values from -6 to 6
- magnetic: bfloat16 [2, 2, 128, 128, 1024], P(None, None, 'order', 'shell'), may hold values from -6 to 6
- legendre: bfloat16 [128, 1024, 1536], P('order'), may hold values from -0.1875 to 0.1875
- quad_weight: float32 [1536], replicated, may hold values from 0.25 to 1.75
- order_table: int32 [128], replicated, may hold values from 0 to 1023, as said below
- field_prev: float32 [2, 128, 128, 1024], P(None, 'order', 'shell'), may hold values from -6 to 6
- rates: float32 [128], replicated, may hold values from 0.05 to 4
- radial_right: float32 [128, 128], replicated, may hold values from -0.5 to 0.5
- radial_left: float32 [128, 128], replicated, may hold values from -0.5 to 0.5
Outputs:
- field_next: float32 [2, 128, 128, 1024], P(None, 'order', 'shell')
The draws below stay inside these ranges and needn't reach their ends.
Inputs may be any that keep to these rules, and one draw needn't show every extreme that they name: `order_table`: slots come in pairs: slot 2 i holds an order m and slot 2 i + 1 holds 1023 - m. All slots hold different orders, and the pair of 0 and 1023 is always present.
All inputs are finite; a program needn't handle non-finite values.
Results may differ from the reference program's by a relative error of at most 0.0058.
Values may be sent and summed in bfloat16 or wider, within the bound.
A program may use at most 128 MiB of HBM per device.

```python
import math
import jax
import jax.numpy as jnp
from jax import lax

L = 1024
NLAT = 1536
NLON = 3072
RADII = 128
ORDERS = 128


def draw_order_table(key, part):
    key = jax.random.fold_in(key, 11)
    first_key = jax.random.fold_in(key, 1)
    second_key = jax.random.fold_in(key, 2)
    candidates = jax.random.permutation(first_key, jnp.arange(1, L // 2, dtype=jnp.int32))
    chosen = jnp.concatenate([jnp.zeros((1,), jnp.int32), candidates[:ORDERS // 2 - 1]])
    chosen = jax.random.permutation(second_key, chosen)
    paired = jnp.stack([chosen, L - 1 - chosen], axis=1)
    return paired.reshape(ORDERS).astype(jnp.int32)


def level_of(rng, dims, shards, smallest, top_value):
    def one(dim, blocks):
        steps = jax.random.uniform(jax.random.fold_in(jax.random.fold_in(rng, 6), dim), (blocks,), jnp.float32, smallest / len(shards), top_value / len(shards))
        return jnp.repeat(jnp.exp(steps), dims[dim] // blocks).reshape((-1,) + (1,) * (len(dims) - dim - 1))

    gain = one(*shards[0])
    for cut in shards[1:]:
        gain = gain * one(*cut)
    return gain


def gaussian(key, shape, width, limit, shards=(), kind=jnp.bfloat16):
    array = jax.random.normal(key, shape, jnp.float32) * width
    if len(shards) > 0:
        array = level_of(key, shape, shards, -0.22, 0.18) * array
    return jnp.clip(array, min=-limit, max=limit).astype(kind)


def setup_inputs(seed: int = 0) -> dict:
    seeds = jax.random.split(jax.random.key(seed), 10)
    return {
        "velocity": gaussian(seeds[0], (2, 2, ORDERS, RADII, L), 1.0, 6.0, ((2, 16), (3, 8))),
        "magnetic": gaussian(seeds[1], (2, 2, ORDERS, RADII, L), 1.0, 6.0, ((2, 16), (3, 8))),
        "legendre": gaussian(seeds[2], (ORDERS, L, NLAT), L ** -0.5, 0.1875, ((0, 16),)),
        "quad_weight": jnp.clip(1.0 + 0.15 * jax.random.normal(seeds[3], (NLAT,), jnp.float32), 0.25, 1.75),
        "order_table": draw_order_table(jax.random.fold_in(seeds[9], 71), 0),
        "field_prev": gaussian(seeds[5], (2, ORDERS, RADII, L), 1.0, 6.0, ((1, 16), (2, 8)), jnp.float32),
        "rates": jnp.clip(jnp.exp(jax.random.uniform(seeds[6], (RADII,), jnp.float32, math.log(0.05), math.log(4.0))), 0.05, 4.0),
        "radial_right": gaussian(seeds[7], (RADII, RADII), RADII ** -0.5, 0.5, (), jnp.float32),
        "radial_left": gaussian(seeds[8], (RADII, RADII), RADII ** -0.5, 0.5, (), jnp.float32),
    }


def phase_rows(order_table, lon_count):
    lon_index = jnp.arange(lon_count, dtype=jnp.int32)
    phase_index = order_table[:, None] * lon_index[None, :] % lon_count
    angles = phase_index.astype(jnp.float32) * (2.0 * math.pi / lon_count)
    return jnp.concatenate([jnp.cos(angles), -jnp.sin(angles)], 0).astype(jnp.bfloat16)

def reference(velocity, magnetic, legendre, quad_weight, order_table, field_prev, rates, radial_right, radial_left):
    coeffs = jnp.concatenate([velocity, magnetic], 0)
    phases = phase_rows(order_table, NLON).astype(jnp.float32)
    table_wide = legendre.astype(jnp.float32)

    def per_radius(radius):
        radius_coeffs = lax.dynamic_index_in_dim(coeffs, radius, 3, keepdims=False)
        synthesis = jnp.einsum('fksl,slt->fkst', radius_coeffs.astype(jnp.float32), table_wide).astype(jnp.bfloat16)
        synthesis = lax.optimization_barrier(synthesis).astype(jnp.float32)
        flattened = synthesis.reshape(4, 2 * ORDERS, NLAT)
        grid_vals = jnp.einsum('fqt,qj->ftj', flattened, phases) / math.sqrt(ORDERS)
        electromotive = (grid_vals[0] * grid_vals[3] - grid_vals[1] * grid_vals[2]).astype(jnp.bfloat16)
        electromotive = lax.optimization_barrier(electromotive).astype(jnp.float32)
        spectra = jnp.einsum('tj,qj->qt', electromotive, phases) / math.sqrt(NLON) * quad_weight[None, :]
        return spectra.astype(jnp.bfloat16)
    spectra = lax.map(per_radius, jnp.arange(RADII, dtype=jnp.int32))
    spectra = lax.optimization_barrier(spectra.reshape(RADII, 2, ORDERS, NLAT)).astype(jnp.float32)
    analysed = jnp.einsum('rkst,slt->ksrl', spectra, table_wide)
    rhs = field_prev + analysed
    mixed_radii = jnp.einsum('qr,ksrl->ksql', radial_right, rhs, precision=lax.Precision.HIGHEST)
    degrees = jnp.arange(L).astype(jnp.float32)
    denom = 1.0 + rates[:, None] + 4.0 * degrees[None, :] * (degrees[None, :] + 1.0) / (L * (L - 1.0))
    scaled = mixed_radii / denom
    return jnp.einsum('rq,ksql->ksrl', radial_left, scaled, precision=lax.Precision.HIGHEST)
```

```python
import functools
import math

import jax
import jax.numpy as jnp
from jax import lax
from jax.experimental import pallas as pl
from jax.experimental.pallas import tpu as pltpu
from jax.sharding import PartitionSpec as P

NLON = 3072
NLAT = 1536
NDEG = 1024
NO = 16
NH = 8
SL = 8
RL = 16
KK = 256
TC = 256
NC = NLAT // TC
JT = 512
GS = 2
NG = SL // GS
GR = GS * 32
BF = jnp.bfloat16
F32 = jnp.float32
STEP = 2.0 * math.pi / NLON


def iota(shape, dim):
    return lax.broadcasted_iota(jnp.int32, shape, dim)


def angle(order, position):
    return ((order * position) % NLON).astype(F32) * STEP


def kernel(
    vel, mag, leg, qw, ot, fprev, rates, right, left, out,
    xv, xm, lv, ybuf, perm, perm_t, ph_t, ph_m, sbuf, rbuf, emf, spec_s, spec_r, acc,
    rhs_s, rhs_r, res_s, res_r, invden,
    x_sem, l_sem, f_sem, own_sem, s1, r1, own2_sem, s2, r2, own3_sem, s3, r3, own4_sem, s4, r4,
):
    me = lax.axis_index("order")
    mh = lax.axis_index("shell")

    def leg_copy(c):
        return pltpu.make_async_copy(
            leg.at[:, :, pl.ds(pl.multiple_of(c * TC, TC), TC)], lv.at[c], l_sem.at[c]
        )

    copy_v = pltpu.make_async_copy(vel, xv, x_sem.at[0])
    copy_m = pltpu.make_async_copy(mag, xm, x_sem.at[1])
    copy_f = [
        pltpu.make_async_copy(fprev.at[k], acc.at[:, pl.ds(16 * k, 16), :], f_sem.at[k])
        for k in range(2)
    ]
    copy_v.start()
    copy_m.start()
    for c in range(NC):
        leg_copy(c).start()
    for k in range(2):
        copy_f[k].start()

    barrier = pltpu.get_barrier_semaphore()

    @pl.loop(1, NO)
    def _(i):
        pl.semaphore_signal(
            barrier, inc=1, device_id=(mh, (me + i) % NO), device_id_type=pl.DeviceIdType.MESH
        )

    @pl.loop(1, NH)
    def _(i):
        pl.semaphore_signal(
            barrier, inc=1, device_id=((mh + i) % NH, me), device_id_type=pl.DeviceIdType.MESH
        )

    row, col = iota((KK, KK), 0), iota((KK, KK), 1)
    source = (row % 8) * 32 + ((row // 8) % 2) * 16 + row // 16
    perm[...] = (col == source).astype(F32).astype(BF)
    source_t = (col % 8) * 32 + ((col // 8) % 2) * 16 + col // 16
    perm_t[...] = (row == source_t).astype(F32).astype(BF)

    copy_v.wait()
    copy_m.wait()
    pl.semaphore_wait(barrier, NO + NH - 2)

    def fields_copy(c, dest):
        return pltpu.make_async_remote_copy(
            src_ref=sbuf.at[c, :, dest],
            dst_ref=rbuf.at[c, :, me],
            send_sem=s1.at[c],
            recv_sem=r1.at[c],
            device_id=(mh, dest),
            device_id_type=pl.DeviceIdType.MESH,
        )

    def own_fields(c):
        return pltpu.make_async_copy(sbuf.at[c, :, me], rbuf.at[c, :, me], own_sem.at[c])

    @pl.loop(0, NC)
    def _(c):
        leg_copy(c).wait()

        @pl.loop(0, SL)
        def _(s):
            x = jnp.concatenate(
                [xv[:, s].reshape(64, NDEG), xm[:, s].reshape(64, NDEG)], axis=0
            )
            y = jnp.dot(x, lv[c, s], preferred_element_type=F32).astype(BF)
            first = pl.multiple_of(s * 32, 32)
            for f in range(4):
                ybuf[f, pl.ds(first, 32), :] = y[32 * f : 32 * f + 32]

        for f in range(4):
            z = jnp.dot(perm[...], ybuf[f], preferred_element_type=F32).astype(BF)
            sbuf[c, f] = z.reshape(NO, 16, TC)

        @pl.loop(1, NO)
        def _(i):
            fields_copy(c, (me + i) % NO).start()

        own_fields(c).start()

    orders = ot[...]
    r0, c0 = iota((KK, 128), 0), iota((KK, 128), 1)
    hit = c0 == (r0 // 16) * 8 + r0 % 8
    order_col = jnp.sum(jnp.where(hit, orders.astype(F32), 0.0), axis=1, keepdims=True)
    order_col = order_col.astype(jnp.int32)
    odd = (r0 // 8) % 2 == 1
    fine = angle(order_col, c0)
    cb, sb = jnp.cos(fine), jnp.sin(fine)
    dm = jnp.where(odd, -sb, cb)
    em = jnp.where(odd, -cb, -sb)
    coarse = angle(order_col, (c0 % (NLON // 128)) * 128)
    ca, sa = jnp.cos(coarse), jnp.sin(coarse)
    for a in range(NLON // 128):
        ph_m[:, a * 128 : a * 128 + 128] = (ca[:, a : a + 1] * dm + sa[:, a : a + 1] * em).astype(BF)

    r1_, c1_ = iota((128, 128), 0), iota((128, 128), 1)
    slot_col = jnp.sum(jnp.where(r1_ == c1_, orders.astype(F32), 0.0), axis=1, keepdims=True)
    r2_, c2_ = iota((128, KK), 0), iota((128, KK), 1)
    hit_t = r2_ == (c2_ // 16) * 8 + c2_ % 8
    order_row = jnp.sum(jnp.where(hit_t, slot_col, 0.0), axis=0, keepdims=True).astype(jnp.int32)
    r3_, c3_ = iota((64, KK), 0), iota((64, KK), 1)
    odd_t = (c3_ // 8) % 2 == 1
    fine_t = angle(order_row, r3_)
    cbt, sbt = jnp.cos(fine_t), jnp.sin(fine_t)
    dt = jnp.where(odd_t, -sbt, cbt)
    et = jnp.where(odd_t, -cbt, -sbt)
    coarse_t = angle(order_row, iota((NLON // 64, KK), 0) * 64)
    cat, sat = jnp.cos(coarse_t), jnp.sin(coarse_t)
    for a in range(NLON // 64):
        ph_t[a * 64 : a * 64 + 64, :] = (cat[a : a + 1] * dt + sat[a : a + 1] * et).astype(BF)

    rate_col = jnp.sum(jnp.where(r1_ == c1_, rates[...], 0.0), axis=1, keepdims=True)
    degree = (mh * 128 + c1_).astype(F32)
    invden[...] = 1.0 / (1.0 + rate_col + 4.0 * degree * (degree + 1.0) / (NDEG * (NDEG - 1.0)))

    scale = 1.0 / (128.0 * math.sqrt(NLON))

    def spectra_copy(c, dest):
        return pltpu.make_async_remote_copy(
            src_ref=spec_s.at[c, dest],
            dst_ref=spec_r.at[c, me],
            send_sem=s2.at[c],
            recv_sem=r2.at[c],
            device_id=(mh, dest),
            device_id_type=pl.DeviceIdType.MESH,
        )

    def own_spectra(c):
        return pltpu.make_async_copy(spec_s.at[c, me], spec_r.at[c, me], own2_sem.at[c])

    def grid_chunk(c):
        own_fields(c).wait()
        several = rbuf.at[c, :, pl.ds(0, NO - 1)]
        pltpu.make_async_copy(several, several, r1.at[c]).wait()

        @pl.loop(0, NLON // JT)
        def _(j):
            rows = pl.ds(pl.multiple_of(j * JT, JT), JT)
            ph = ph_t[rows, :]
            g = [
                jnp.dot(ph, rbuf[c, f].reshape(KK, TC), preferred_element_type=F32)
                for f in range(4)
            ]
            emf[rows, :] = (g[0] * g[3] - g[1] * g[2]).astype(BF)

        spec = jnp.dot(ph_m[...], emf[...], preferred_element_type=F32)
        weight = qw[:, pl.ds(pl.multiple_of(c * TC, TC), TC)] * scale
        spec_s[c] = (spec * weight).astype(BF).reshape(NO, 16, TC)

        @pl.loop(1, NO)
        def _(i):
            spectra_copy(c, (me + i) % NO).start()

        own_spectra(c).start()

    def spectra_rows(c):
        own_spectra(c).wait()
        several = spec_r.at[c, pl.ds(0, NO - 1)]
        pltpu.make_async_copy(several, several, r2.at[c]).wait()
        z = jnp.dot(perm_t[...], spec_r[c].reshape(KK, TC), preferred_element_type=F32)
        ybuf[0] = z.astype(BF)

    def analyse_slot(c, s):
        part = lax.dot_general(
            ybuf[0, pl.ds(pl.multiple_of(s * 32, 32), 32), :],
            lv[c, s],
            (((1,), (1,)), ((), ())),
            preferred_element_type=F32,
        )
        total = acc[s] + part
        acc[s] = total
        return total

    for k in range(2):
        copy_f[k].wait()

    grid_chunk(0)

    @pl.loop(1, NC)
    def _(c):
        grid_chunk(c)
        spectra_rows(c - 1)

        @pl.loop(0, SL)
        def _(s):
            analyse_slot(c - 1, s)

    spectra_rows(NC - 1)

    def rhs_copy(g, dest):
        return pltpu.make_async_remote_copy(
            src_ref=rhs_s.at[g, dest],
            dst_ref=rhs_r.at[g, mh],
            send_sem=s3.at[g],
            recv_sem=r3.at[g],
            device_id=(dest, me),
            device_id_type=pl.DeviceIdType.MESH,
        )

    def own_rhs(g):
        return pltpu.make_async_copy(rhs_s.at[g, mh], rhs_r.at[g, mh], own3_sem.at[g])

    def result_copy(g, dest):
        return pltpu.make_async_remote_copy(
            src_ref=res_s.at[g, dest],
            dst_ref=res_r.at[g, mh],
            send_sem=s4.at[g],
            recv_sem=r4.at[g],
            device_id=(dest, me),
            device_id_type=pl.DeviceIdType.MESH,
        )

    def own_result(g):
        return pltpu.make_async_copy(res_s.at[g, mh], res_r.at[g, mh], own4_sem.at[g])

    @pl.loop(0, NG)
    def _(g):
        @pl.loop(0, GS)
        def _(i):
            total = analyse_slot(NC - 1, g * GS + i).astype(BF)
            rows = pl.ds(pl.multiple_of(i * 32, 32), 32)
            for d in range(NH):
                rhs_s[g, d, rows, :] = total[:, d * 128 : d * 128 + 128]

        @pl.loop(1, NH)
        def _(i):
            rhs_copy(g, (mh + i) % NH).start()

        own_rhs(g).start()

    @pl.loop(0, NG)
    def _(g):
        own_rhs(g).wait()
        several = rhs_r.at[g, pl.ds(0, NH - 1)]
        pltpu.make_async_copy(several, several, r3.at[g]).wait()
        x = jnp.concatenate(
            [rhs_r[g, :, 16 * b : 16 * b + 16, :].reshape(128, 128) for b in range(2 * GS)], axis=1
        ).astype(F32)
        mixed = jnp.dot(right[...], x, precision=lax.Precision.HIGHEST, preferred_element_type=F32)
        scaled = mixed * jnp.concatenate([invden[...]] * (2 * GS), axis=1)
        res = jnp.dot(left[...], scaled, precision=lax.Precision.HIGHEST, preferred_element_type=F32)
        res = res.astype(BF)
        for b in range(2 * GS):
            res_s[g, :, 16 * b : 16 * b + 16, :] = res[:, 128 * b : 128 * b + 128].reshape(8, 16, 128)

        @pl.loop(1, NH)
        def _(i):
            result_copy(g, (mh + i) % NH).start()

        own_result(g).start()

    @pl.loop(0, NG)
    def _(g):
        own_result(g).wait()
        several = res_r.at[g, pl.ds(0, NH - 1)]
        pltpu.make_async_copy(several, several, r4.at[g]).wait()
        for i in range(GS):
            for k in range(2):
                for d in range(NH):
                    out[k, g * GS + i, :, d * 128 : d * 128 + 128] = res_r[
                        g, d, (2 * i + k) * 16 : (2 * i + k) * 16 + 16, :
                    ].astype(F32)

    @pl.loop(0, NC)
    def _(c):
        several = sbuf.at[c, :, pl.ds(0, NO - 1)]
        pltpu.make_async_copy(several, several, s1.at[c]).wait()
        several = spec_s.at[c, pl.ds(0, NO - 1)]
        pltpu.make_async_copy(several, several, s2.at[c]).wait()

    @pl.loop(0, NG)
    def _(g):
        several = rhs_s.at[g, pl.ds(0, NH - 1)]
        pltpu.make_async_copy(several, several, s3.at[g]).wait()
        several = res_s.at[g, pl.ds(0, NH - 1)]
        pltpu.make_async_copy(several, several, s4.at[g]).wait()


def body(
    velocity, magnetic, legendre, quad_weight, order_table, field_prev, rates, radial_right, radial_left
):
    hbm = pl.BlockSpec(memory_space=pl.ANY)
    vmem = pl.BlockSpec(memory_space=pltpu.VMEM)
    sem = pltpu.SemaphoreType.DMA
    return pl.pallas_call(
        kernel,
        out_shape=jax.ShapeDtypeStruct((2, SL, RL, NDEG), F32),
        in_specs=[hbm, hbm, hbm, vmem, vmem, hbm, vmem, vmem, vmem],
        out_specs=vmem,
        scratch_shapes=[
            pltpu.VMEM((4, SL, RL, NDEG), BF),
            pltpu.VMEM((4, SL, RL, NDEG), BF),
            pltpu.VMEM((NC, SL, NDEG, TC), BF),
            pltpu.VMEM((4, KK, TC), BF),
            pltpu.VMEM((KK, KK), BF),
            pltpu.VMEM((KK, KK), BF),
            pltpu.VMEM((NLON, KK), BF),
            pltpu.VMEM((KK, NLON), BF),
            pltpu.VMEM((NC, 4, NO, 16, TC), BF),
            pltpu.VMEM((NC, 4, NO, 16, TC), BF),
            pltpu.VMEM((NLON, TC), BF),
            pltpu.VMEM((NC, NO, 16, TC), BF),
            pltpu.VMEM((NC, NO, 16, TC), BF),
            pltpu.VMEM((SL, 32, NDEG), F32),
            pltpu.VMEM((NG, NH, GR, 128), BF),
            pltpu.VMEM((NG, NH, GR, 128), BF),
            pltpu.VMEM((NG, NH, GR, 128), BF),
            pltpu.VMEM((NG, NH, GR, 128), BF),
            pltpu.VMEM((128, 128), F32),
            sem((2,)),
            sem((NC,)),
            sem((2,)),
            sem((NC,)),
            sem((NC,)),
            sem((NC,)),
            sem((NC,)),
            sem((NC,)),
            sem((NC,)),
            sem((NG,)),
            sem((NG,)),
            sem((NG,)),
            sem((NG,)),
            sem((NG,)),
            sem((NG,)),
        ],
        compiler_params=pltpu.CompilerParams(
            collective_id=0, has_side_effects=True, vmem_limit_bytes=58 * 1024 * 1024
        ),
        cost_estimate=pl.CostEstimate(
            flops=18_000_000_000, bytes_accessed=32_000_000, transcendentals=0
        ),
    )(
        velocity.reshape(4, SL, RL, NDEG),
        magnetic.reshape(4, SL, RL, NDEG),
        legendre,
        quad_weight.reshape(1, NLAT),
        order_table.reshape(1, 128),
        field_prev,
        rates.reshape(1, 128),
        radial_right,
        radial_left,
    )


def solution(mesh):
    return jax.shard_map(
        body,
        mesh=mesh,
        in_specs=(
            P(None, None, "order", "shell", None),
            P(None, None, "order", "shell", None),
            P("order", None, None),
            P(),
            P(),
            P(None, "order", "shell", None),
            P(),
            P(),
            P(),
        ),
        out_specs=P(None, "order", "shell", None),
        check_vma=False,
    )
```

```python
import math

import jax
import jax.numpy as jnp
from jax import lax
from jax.experimental import pallas as pl
from jax.experimental.pallas import tpu as pltpu
from jax.sharding import PartitionSpec as P

NLON = 3072
NLAT = 1536
NDEG = 1024
NO = 16
NX = 4
NH = 8
SL = 8
RL = 16
KK = 256
TC = 256
NC = NLAT // TC
JT = 512
LB = 256
NB = NDEG // LB
NP = 2 * NO
BF = jnp.bfloat16
F32 = jnp.float32
STEP = 2.0 * math.pi / NLON
MESH = pl.DeviceIdType.MESH


def iota(shape, dim):
    return lax.broadcasted_iota(jnp.int32, shape, dim)


def angle(order, position):
    return ((order * position) % NLON).astype(F32) * STEP


def slot_of(q):
    return ((q % 16) // 8) * 4 + q % 4


def part_of(q):
    return (q // 4) % 2


def split(x):
    high = x.astype(BF)
    return high, (x - high.astype(F32)).astype(BF)


def all_but_one(ref, sem):
    pltpu.make_async_copy(ref, ref, sem).wait()


def kernel(
    vel, mag, leg, qw, ot, fprev, rates, right, left, out,
    xv, xm, lv, fp, fp_s, fp_r, ybuf, perm, perm2, ph_t, ph_m, sbuf, rbuf, emf, spec_s, spec_r,
    fwd_s, fwd_r, acc, res_s, invden, right_c, left_c,
    x_sem, l_sem, f_sem, o0, s0, r0, o1, s1, r1, o2, s2, r2, o3, s3, r3, o4, s4, r4,
):
    me = lax.axis_index("order")
    mh = lax.axis_index("shell")
    my = mh // NX
    mx = mh % NX
    mp = my * NO + me

    def leg_copy(c, s):
        return pltpu.make_async_copy(
            leg.at[s, :, pl.ds(pl.multiple_of(c * TC, TC), TC)], lv.at[c, s], l_sem.at[c, s]
        )

    copy_v = pltpu.make_async_copy(vel, xv, x_sem.at[0])
    copy_m = pltpu.make_async_copy(mag, xm, x_sem.at[1])
    copy_f = pltpu.make_async_copy(fprev, fp, f_sem)
    copy_f.start()
    copy_v.start()
    copy_m.start()

    @pl.loop(0, NC)
    def _(c):
        @pl.loop(0, SL)
        def _(s):
            leg_copy(c, s).start()

    barrier = pltpu.get_barrier_semaphore()

    @pl.loop(1, NP)
    def _(i):
        p = (mp + i) % NP
        pl.semaphore_signal(
            barrier, inc=1, device_id=((p // NO) * NX + mx, p % NO), device_id_type=MESH
        )

    @pl.loop(1, NX)
    def _(i):
        x = (mx + i) % NX
        for y in range(2):
            pl.semaphore_signal(barrier, inc=1, device_id=(y * NX + x, me), device_id_type=MESH)

    row, col = iota((KK, KK), 0), iota((KK, KK), 1)
    source = slot_of(row) * 32 + part_of(row) * 16 + row // 16
    perm[...] = (col == source).astype(F32).astype(BF)
    row, col = iota((512, 512), 0), iota((512, 512), 1)
    source = (row % 32) * 16 + (row // 256) * 8 + ((row // 32) % 2) * 4 + (row % 256) // 64
    perm2[...] = (col == source).astype(F32).astype(BF)

    def prev_copy(dest):
        return pltpu.make_async_remote_copy(
            src_ref=fp_s.at[dest], dst_ref=fp_r.at[mh], send_sem=s0, recv_sem=r0,
            device_id=(dest, me), device_id_type=MESH,
        )

    own_prev = pltpu.make_async_copy(fp_s.at[mh], fp_r.at[mh], o0)
    copy_f.wait()
    for k in range(2):
        fp_s[:, 16 * k : 16 * k + 16, :] = fp[k].astype(BF)
    pl.semaphore_wait(barrier, NP - 1 + 2 * (NX - 1))

    @pl.loop(1, NH)
    def _(i):
        prev_copy((mh + i) % NH).start()

    own_prev.start()
    copy_v.wait()
    copy_m.wait()

    def fields_copy(c, dest):
        return pltpu.make_async_remote_copy(
            src_ref=sbuf.at[c, :, dest], dst_ref=rbuf.at[c, :, me],
            send_sem=s1.at[c], recv_sem=r1.at[c],
            device_id=(mh, dest), device_id_type=MESH,
        )

    def own_fields(c):
        return pltpu.make_async_copy(sbuf.at[c, :, me], rbuf.at[c, :, me], o1.at[c])

    @pl.loop(0, NC)
    def _(c):
        @pl.loop(0, SL)
        def _(s):
            leg_copy(c, s).wait()
            x = jnp.concatenate(
                [xv[:, s].reshape(64, NDEG), xm[:, s].reshape(64, NDEG)], axis=0
            )
            y = jnp.dot(x, lv[c, s], preferred_element_type=F32).astype(BF)
            first = pl.multiple_of(s * 32, 32)
            for f in range(4):
                ybuf[f, pl.ds(first, 32), :] = y[32 * f : 32 * f + 32]

        for f in range(4):
            z = jnp.dot(perm[...], ybuf[f], preferred_element_type=F32).astype(BF)
            sbuf[c, f] = z.reshape(NO, 16, TC)

        @pl.loop(1, NO)
        def _(i):
            fields_copy(c, (me + i) % NO).start()

        own_fields(c).start()

    orders = ot[...].astype(F32)
    ra, ca = iota((KK, 128), 0), iota((KK, 128), 1)
    hit = ca == (ra // 16) * 8 + slot_of(ra)
    order_col = jnp.sum(jnp.where(hit, orders, 0.0), axis=1, keepdims=True).astype(jnp.int32)
    odd = part_of(ra) == 1
    fine = angle(order_col, ca)
    cb, sb = jnp.cos(fine), jnp.sin(fine)
    dm = jnp.where(odd, -sb, cb)
    em = jnp.where(odd, -cb, -sb)
    coarse = angle(order_col, (ca % (NLON // 128)) * 128)
    cc, sc = jnp.cos(coarse), jnp.sin(coarse)
    for a in range(NLON // 128):
        ph_m[:, a * 128 : a * 128 + 128] = (cc[:, a : a + 1] * dm + sc[:, a : a + 1] * em).astype(BF)

    rb, cb2 = iota((128, 128), 0), iota((128, 128), 1)
    slot_col = jnp.sum(jnp.where(rb == cb2, orders, 0.0), axis=1, keepdims=True)
    rd, cd = iota((128, KK), 0), iota((128, KK), 1)
    hit_t = rd == (cd // 16) * 8 + slot_of(cd)
    order_row = jnp.sum(jnp.where(hit_t, slot_col, 0.0), axis=0, keepdims=True).astype(jnp.int32)
    re, ce = iota((64, KK), 0), iota((64, KK), 1)
    odd_t = part_of(ce) == 1
    fine_t = angle(order_row, re)
    cbt, sbt = jnp.cos(fine_t), jnp.sin(fine_t)
    dt = jnp.where(odd_t, -sbt, cbt)
    et = jnp.where(odd_t, -cbt, -sbt)
    coarse_t = angle(order_row, iota((NLON // 64, KK), 0) * 64)
    cat, sat = jnp.cos(coarse_t), jnp.sin(coarse_t)
    for a in range(NLON // 64):
        ph_t[a * 64 : a * 64 + 64, :] = (cat[a : a + 1] * dt + sat[a : a + 1] * et).astype(BF)

    rate_col = jnp.sum(jnp.where(rb == cb2, rates[...], 0.0), axis=1, keepdims=True)
    degree = iota((128, NDEG), 1).astype(F32)
    invden[...] = 1.0 / (1.0 + rate_col + 4.0 * degree * (degree + 1.0) / (NDEG * (NDEG - 1.0)))
    for factor, halves in ((right, right_c), (left, left_c)):
        high, low = split(factor[...])
        halves[...] = jnp.concatenate([high, low, high], axis=1)

    scale = 1.0 / (128.0 * math.sqrt(NLON))

    def spectra_copy(c, p):
        return pltpu.make_async_remote_copy(
            src_ref=spec_s.at[c, p % NO, p // NO], dst_ref=spec_r.at[c, mp],
            send_sem=s2.at[c], recv_sem=r2.at[c],
            device_id=((p // NO) * NX + mx, p % NO), device_id_type=MESH,
        )

    def own_spectra(c):
        return pltpu.make_async_copy(spec_s.at[c, me, my], spec_r.at[c, mp], o2.at[c])

    @pl.loop(0, NC)
    def _(c):
        own_fields(c).wait()
        all_but_one(rbuf.at[c, :, pl.ds(0, NO - 1)], r1.at[c])

        @pl.loop(0, NLON // JT)
        def _(j):
            rows = pl.ds(pl.multiple_of(j * JT, JT), JT)
            ph = ph_t[rows, :]
            g = [
                jnp.dot(ph, rbuf[c, f].reshape(KK, TC), preferred_element_type=F32)
                for f in range(4)
            ]
            emf[rows, :] = (g[0] * g[3] - g[1] * g[2]).astype(BF)

        spec = jnp.dot(ph_m[...], emf[...], preferred_element_type=F32)
        halves = []
        for th in range(2):
            weight = qw[pl.ds(2 * c + th, 1), :] * scale
            halves.append((spec[:, 128 * th : 128 * th + 128] * weight).reshape(NO, 2, 8, 128))
        spec_s[c] = jnp.concatenate(halves, axis=2).astype(BF)

        @pl.loop(1, NP)
        def _(i):
            spectra_copy(c, (mp + i) % NP).start()

        own_spectra(c).start()

    def forward_copy(c, x):
        return pltpu.make_async_remote_copy(
            src_ref=fwd_s.at[c, x], dst_ref=fwd_r.at[c, mx],
            send_sem=s3.at[c], recv_sem=r3.at[c],
            device_id=(my * NX + x, me), device_id_type=MESH,
        )

    def own_forward(c):
        return pltpu.make_async_copy(fwd_s.at[c, mx], fwd_r.at[c, mx], o3.at[c])

    def forward(c):
        own_spectra(c).wait()
        all_but_one(spec_r.at[c, pl.ds(0, NP - 1)], r2.at[c])
        z = jnp.dot(perm2[...], spec_r[c].reshape(512, 128), preferred_element_type=F32).astype(BF)
        fwd_s[c] = jnp.concatenate([z[:256], z[256:]], axis=1).reshape(NX, 64, TC)

        @pl.loop(1, NX)
        def _(i):
            forward_copy(c, (mx + i) % NX).start()

        own_forward(c).start()

    def analysed(c, lb):
        return lax.dot_general(
            fwd_r[c].reshape(256, TC),
            lv[c, mh, pl.ds(pl.multiple_of(lb * LB, LB), LB), :],
            (((1,), (1,)), ((), ())),
            preferred_element_type=F32,
        )

    def forwarded(c):
        own_forward(c).wait()
        all_but_one(fwd_r.at[c, pl.ds(0, NX - 1)], r3.at[c])

    own_prev.wait()
    all_but_one(fp_r.at[pl.ds(0, NH - 1)], r0)

    for h in range(NH):
        for k in range(2):
            first = (h % NX) * 64 + k * 32 + (h // NX) * 16
            acc[first : first + 16, :] = fp_r[h, 16 * k : 16 * k + 16, :].astype(F32)

    forward(0)

    @pl.loop(1, NC)
    def _(c):
        forward(c)
        forwarded(c - 1)
        for lb in range(NB):
            acc[:, lb * LB : lb * LB + LB] += analysed(c - 1, lb)

    forwarded(NC - 1)

    def result_copy(b, dest):
        return pltpu.make_async_remote_copy(
            src_ref=res_s.at[b, dest],
            dst_ref=out.at[:, mh, :, pl.ds(pl.multiple_of(b * LB, LB), LB)],
            send_sem=s4.at[b], recv_sem=r4.at[b],
            device_id=(dest, me), device_id_type=MESH,
        )

    def own_result(b):
        return pltpu.make_async_copy(
            res_s.at[b, mh], out.at[:, mh, :, pl.ds(pl.multiple_of(b * LB, LB), LB)], o4.at[b]
        )

    @pl.loop(0, NB)
    def _(b):
        lanes = pl.ds(pl.multiple_of(b * LB, LB), LB)
        total = acc[:, lanes] + analysed(NC - 1, b)
        rhs = jnp.concatenate(
            [
                jnp.concatenate(
                    [
                        total[(h % NX) * 64 + k * 32 + (h // NX) * 16 :][:16]
                        for h in range(NH)
                    ],
                    axis=0,
                )
                for k in range(2)
            ],
            axis=1,
        )
        high, low = split(rhs)
        mixed = jnp.dot(
            right_c[...], jnp.concatenate([high, high, low], axis=0), preferred_element_type=F32
        )
        damp = invden[:, lanes]
        high, low = split(mixed * jnp.concatenate([damp, damp], axis=1))
        res = jnp.dot(
            left_c[...], jnp.concatenate([high, high, low], axis=0), preferred_element_type=F32
        ).astype(BF)
        for k in range(2):
            res_s[b, :, k] = res[:, k * LB : k * LB + LB].reshape(NH, RL, LB)

        @pl.loop(1, NH)
        def _(i):
            result_copy(b, (mh + i) % NH).start()

        own_result(b).start()

    all_but_one(fp_s.at[pl.ds(0, NH - 1)], s0)

    @pl.loop(0, NC)
    def _(c):
        all_but_one(sbuf.at[c, :, pl.ds(0, NO - 1)], s1.at[c])
        all_but_one(spec_r.at[c, pl.ds(0, NP - 1)], s2.at[c])
        all_but_one(fwd_s.at[c, pl.ds(0, NX - 1)], s3.at[c])

    @pl.loop(0, NB)
    def _(b):
        all_but_one(res_s.at[b, pl.ds(0, NH - 1)], s4.at[b])
        own_result(b).wait()
        all_but_one(res_s.at[b, pl.ds(0, NH - 1)], r4.at[b])


def body(
    velocity, magnetic, legendre, quad_weight, order_table, field_prev, rates, radial_right, radial_left
):
    hbm = pl.BlockSpec(memory_space=pl.ANY)
    vmem = pl.BlockSpec(memory_space=pltpu.VMEM)
    sem = pltpu.SemaphoreType.DMA
    result = pl.pallas_call(
        kernel,
        out_shape=jax.ShapeDtypeStruct((2, SL, RL, NDEG), BF),
        in_specs=[hbm, hbm, hbm, vmem, vmem, hbm, vmem, vmem, vmem],
        out_specs=hbm,
        scratch_shapes=[
            pltpu.VMEM((4, SL, RL, NDEG), BF),
            pltpu.VMEM((4, SL, RL, NDEG), BF),
            pltpu.VMEM((NC, SL, NDEG, TC), BF),
            pltpu.VMEM((2, SL, RL, NDEG), F32),
            pltpu.VMEM((NH, 32, NDEG), BF),
            pltpu.VMEM((NH, 32, NDEG), BF),
            pltpu.VMEM((4, KK, TC), BF),
            pltpu.VMEM((KK, KK), BF),
            pltpu.VMEM((512, 512), BF),
            pltpu.VMEM((NLON, KK), BF),
            pltpu.VMEM((KK, NLON), BF),
            pltpu.VMEM((NC, 4, NO, 16, TC), BF),
            pltpu.VMEM((NC, 4, NO, 16, TC), BF),
            pltpu.VMEM((NLON, TC), BF),
            pltpu.VMEM((NC, NO, 2, 16, 128), BF),
            pltpu.VMEM((NC, NP, 16, 128), BF),
            pltpu.VMEM((NC, NX, 64, TC), BF),
            pltpu.VMEM((NC, NX, 64, TC), BF),
            pltpu.VMEM((256, NDEG), F32),
            pltpu.VMEM((NB, NH, 2, RL, LB), BF),
            pltpu.VMEM((128, NDEG), F32),
            pltpu.VMEM((128, 384), BF),
            pltpu.VMEM((128, 384), BF),
            sem((2,)),
            sem((NC, SL)),
            sem,
            sem, sem, sem,
            sem((NC,)), sem((NC,)), sem((NC,)),
            sem((NC,)), sem((NC,)), sem((NC,)),
            sem((NC,)), sem((NC,)), sem((NC,)),
            sem((NB,)), sem((NB,)), sem((NB,)),
        ],
        compiler_params=pltpu.CompilerParams(
            collective_id=0, has_side_effects=True, vmem_limit_bytes=58 * 1024 * 1024
        ),
        cost_estimate=pl.CostEstimate(
            flops=18_000_000_000, bytes_accessed=32_000_000, transcendentals=0
        ),
    )(
        velocity.reshape(4, SL, RL, NDEG),
        magnetic.reshape(4, SL, RL, NDEG),
        legendre,
        quad_weight.reshape(NLAT // 128, 128),
        order_table.reshape(1, 128),
        field_prev,
        rates.reshape(1, 128),
        radial_right,
        radial_left,
    )
    return result.astype(F32)


def solution(mesh):
    return jax.shard_map(
        body,
        mesh=mesh,
        in_specs=(
            P(None, None, "order", "shell", None),
            P(None, None, "order", "shell", None),
            P("order", None, None),
            P(),
            P(),
            P(None, "order", "shell", None),
            P(),
            P(),
            P(),
        ),
        out_specs=P(None, "order", "shell", None),
        check_vma=False,
    )
```

```python
import math

import jax
import jax.numpy as jnp
from jax import lax
from jax.experimental import pallas as pl
from jax.experimental.pallas import tpu as pltpu
from jax.sharding import PartitionSpec as P

NLON = 3072
NLAT = 1536
NDEG = 1024
NO = 16
NX = 4
NH = 8
SL = 8
RL = 16
KK = 256
TC = 256
NC = NLAT // TC
JT = 1536
LB = 256
NB = NDEG // LB
NP = 2 * NO
BF = jnp.bfloat16
F32 = jnp.float32
STEP = 2.0 * math.pi / NLON
MESH = pl.DeviceIdType.MESH


def iota(shape, dim):
    return lax.broadcasted_iota(jnp.int32, shape, dim)


def angle(order, position):
    return ((order * position) % NLON).astype(F32) * STEP


def slot_of(q):
    return ((q % 16) // 8) * 4 + q % 4


def part_of(q):
    return (q // 4) % 2


def split(x):
    high = x.astype(BF)
    return high, (x - high.astype(F32)).astype(BF)


def all_but_one(ref, sem):
    pltpu.make_async_copy(ref, ref, sem).wait()


def kernel(
    vel, mag, leg, qw, ot, fprev, rates, right, left, out,
    xv, xm, lv, fp, fp_s, fp_r, ybuf, perm, perm2, ph_t, ph_m, sbuf, rbuf, emf, spec_s, spec_r,
    fwd_s, fwd_r, acc, res_s, invden, right_c, left_c,
    x_sem, l_sem, f_sem, o0, s0, r0, o1, s1, r1, o2, s2, r2, o3, s3, r3, o4, s4, r4,
):
    me = lax.axis_index("order")
    mh = lax.axis_index("shell")
    my = mh // NX
    mx = mh % NX
    mp = my * NO + me

    barrier = pltpu.get_barrier_semaphore()

    @pl.loop(1, NP)
    def _(i):
        p = (mp + i) % NP
        pl.semaphore_signal(
            barrier, inc=1, device_id=((p // NO) * NX + mx, p % NO), device_id_type=MESH
        )

    @pl.loop(1, NX)
    def _(i):
        x = (mx + i) % NX
        for y in range(2):
            pl.semaphore_signal(barrier, inc=1, device_id=(y * NX + x, me), device_id_type=MESH)

    def leg_copy(c, s):
        return pltpu.make_async_copy(
            leg.at[s, :, pl.ds(pl.multiple_of(c * TC, TC), TC)], lv.at[c, s], l_sem.at[c, s]
        )

    copy_v = pltpu.make_async_copy(vel, xv, x_sem.at[0])
    copy_m = pltpu.make_async_copy(mag, xm, x_sem.at[1])
    copy_f = pltpu.make_async_copy(fprev, fp, f_sem)
    copy_f.start()
    copy_v.start()
    copy_m.start()

    @pl.loop(0, NC)
    def _(c):
        @pl.loop(0, SL)
        def _(s):
            leg_copy(c, s).start()

    row, col = iota((KK, KK), 0), iota((KK, KK), 1)
    source = slot_of(row) * 32 + part_of(row) * 16 + row // 16
    perm[...] = (col == source).astype(F32).astype(BF)
    row, col = iota((512, 512), 0), iota((512, 512), 1)
    source = (row % 32) * 16 + (row // 256) * 8 + ((row // 32) % 2) * 4 + (row % 256) // 64
    perm2[...] = (col == source).astype(F32).astype(BF)

    def prev_copy(dest):
        return pltpu.make_async_remote_copy(
            src_ref=fp_s.at[dest], dst_ref=fp_r.at[mh], send_sem=s0, recv_sem=r0,
            device_id=(dest, me), device_id_type=MESH,
        )

    own_prev = pltpu.make_async_copy(fp_s.at[mh], fp_r.at[mh], o0)

    def fields_copy(c, dest):
        return pltpu.make_async_remote_copy(
            src_ref=sbuf.at[c, :, dest], dst_ref=rbuf.at[c, :, me],
            send_sem=s1.at[c], recv_sem=r1.at[c],
            device_id=(mh, dest), device_id_type=MESH,
        )

    def own_fields(c):
        return pltpu.make_async_copy(sbuf.at[c, :, me], rbuf.at[c, :, me], o1.at[c])

    def synthesise(c):
        @pl.loop(0, SL)
        def _(s):
            leg_copy(c, s).wait()
            x = jnp.concatenate(
                [xv[:, s].reshape(64, NDEG), xm[:, s].reshape(64, NDEG)], axis=0
            )
            y = jnp.dot(x, lv[c, s], preferred_element_type=F32).astype(BF)
            first = pl.multiple_of(s * 32, 32)
            for f in range(4):
                ybuf[f, pl.ds(first, 32), :] = y[32 * f : 32 * f + 32]

        for f in range(4):
            z = jnp.dot(perm[...], ybuf[f], preferred_element_type=F32).astype(BF)
            sbuf[c, f] = z.reshape(NO, 16, TC)

    def send_fields(c):
        @pl.loop(1, NO)
        def _(i):
            fields_copy(c, (me + i) % NO).start()

        own_fields(c).start()

    copy_v.wait()
    copy_m.wait()
    synthesise(0)
    pl.semaphore_wait(barrier, NP - 1 + 2 * (NX - 1))
    send_fields(0)
    copy_f.wait()
    for k in range(2):
        fp_s[:, 16 * k : 16 * k + 16, :] = fp[k].astype(BF)

    @pl.loop(1, NH)
    def _(i):
        prev_copy((mh + i) % NH).start()

    own_prev.start()
    synthesise(1)
    send_fields(1)
    synthesise(2)
    send_fields(2)
    synthesise(3)
    send_fields(3)
    synthesise(4)

    orders = ot[...].astype(F32)
    ra, ca = iota((KK, 128), 0), iota((KK, 128), 1)
    hit = ca == (ra // 16) * 8 + slot_of(ra)
    order_col = jnp.sum(jnp.where(hit, orders, 0.0), axis=1, keepdims=True).astype(jnp.int32)
    odd = part_of(ra) == 1
    fine = angle(order_col, ca)
    cb, sb = jnp.cos(fine), jnp.sin(fine)
    dm = jnp.where(odd, -sb, cb)
    em = jnp.where(odd, -cb, -sb)
    coarse = angle(order_col, (ca % (NLON // 128)) * 128)
    cc, sc = jnp.cos(coarse), jnp.sin(coarse)
    for a in range(NLON // 128):
        ph_m[:, a * 128 : a * 128 + 128] = (cc[:, a : a + 1] * dm + sc[:, a : a + 1] * em).astype(BF)

    rb, cb2 = iota((128, 128), 0), iota((128, 128), 1)
    slot_col = jnp.sum(jnp.where(rb == cb2, orders, 0.0), axis=1, keepdims=True)
    rd, cd = iota((128, KK), 0), iota((128, KK), 1)
    hit_t = rd == (cd // 16) * 8 + slot_of(cd)
    order_row = jnp.sum(jnp.where(hit_t, slot_col, 0.0), axis=0, keepdims=True).astype(jnp.int32)
    re, ce = iota((64, KK), 0), iota((64, KK), 1)
    odd_t = part_of(ce) == 1
    fine_t = angle(order_row, re)
    cbt, sbt = jnp.cos(fine_t), jnp.sin(fine_t)
    dt = jnp.where(odd_t, -sbt, cbt)
    et = jnp.where(odd_t, -cbt, -sbt)
    coarse_t = angle(order_row, iota((NLON // 64, KK), 0) * 64)
    cat, sat = jnp.cos(coarse_t), jnp.sin(coarse_t)
    for a in range(NLON // 64):
        ph_t[a * 64 : a * 64 + 64, :] = (cat[a : a + 1] * dt + sat[a : a + 1] * et).astype(BF)

    rate_col = jnp.sum(jnp.where(rb == cb2, rates[...], 0.0), axis=1, keepdims=True)
    degree = iota((128, NDEG), 1).astype(F32)
    invden[...] = 1.0 / (1.0 + rate_col + 4.0 * degree * (degree + 1.0) / (NDEG * (NDEG - 1.0)))
    for factor, halves in ((right, right_c), (left, left_c)):
        high, low = split(factor[...])
        halves[...] = jnp.concatenate([high, low, high], axis=1)

    scale = 1.0 / (128.0 * math.sqrt(NLON))

    def spectra_copy(c, p):
        return pltpu.make_async_remote_copy(
            src_ref=spec_s.at[c, p % NO, p // NO], dst_ref=spec_r.at[c, mp],
            send_sem=s2.at[c], recv_sem=r2.at[c],
            device_id=((p // NO) * NX + mx, p % NO), device_id_type=MESH,
        )

    def own_spectra(c):
        return pltpu.make_async_copy(spec_s.at[c, me, my], spec_r.at[c, mp], o2.at[c])

    def wait_fields(c):
        own_fields(c).wait()
        all_but_one(rbuf.at[c, :, pl.ds(0, NO - 1)], r1.at[c])

    def grid_chunk(c):
        @pl.loop(0, NLON // JT)
        def _(j):
            rows = pl.ds(pl.multiple_of(j * JT, JT), JT)
            ph = ph_t[rows, :]
            g = [
                jnp.dot(ph, rbuf[c, f].reshape(KK, TC), preferred_element_type=F32)
                for f in range(4)
            ]
            emf[rows, :] = (g[0] * g[3] - g[1] * g[2]).astype(BF)

        spec = jnp.dot(ph_m[...], emf[...], preferred_element_type=F32)
        halves = []
        for th in range(2):
            weight = qw[pl.ds(2 * c + th, 1), :] * scale
            halves.append((spec[:, 128 * th : 128 * th + 128] * weight).reshape(NO, 2, 8, 128))
        spec_s[c] = jnp.concatenate(halves, axis=2).astype(BF)

        @pl.loop(1, NP)
        def _(i):
            spectra_copy(c, (mp + i) % NP).start()

        own_spectra(c).start()

    def forward_copy(c, x):
        return pltpu.make_async_remote_copy(
            src_ref=fwd_s.at[c, x], dst_ref=fwd_r.at[c, mx],
            send_sem=s3.at[c], recv_sem=r3.at[c],
            device_id=(my * NX + x, me), device_id_type=MESH,
        )

    def own_forward(c):
        return pltpu.make_async_copy(fwd_s.at[c, mx], fwd_r.at[c, mx], o3.at[c])

    def forward(c):
        own_spectra(c).wait()
        all_but_one(spec_r.at[c, pl.ds(0, NP - 1)], r2.at[c])
        z = jnp.dot(perm2[...], spec_r[c].reshape(512, 128), preferred_element_type=F32).astype(BF)
        fwd_s[c] = jnp.concatenate([z[:256], z[256:]], axis=1).reshape(NX, 64, TC)

        @pl.loop(1, NX)
        def _(i):
            forward_copy(c, (mx + i) % NX).start()

        own_forward(c).start()

    def analysed(c, lb):
        return lax.dot_general(
            fwd_r[c].reshape(256, TC),
            lv[c, mh, pl.ds(pl.multiple_of(lb * LB, LB), LB), :],
            (((1,), (1,)), ((), ())),
            preferred_element_type=F32,
        )

    def forwarded(c):
        own_forward(c).wait()
        all_but_one(fwd_r.at[c, pl.ds(0, NX - 1)], r3.at[c])

    def analyse(c):
        forwarded(c)
        for lb in range(NB):
            acc[:, lb * LB : lb * LB + LB] += analysed(c, lb)

    @pl.loop(0, NC)
    def _(c):
        wait_fields(c)

        @pl.when(c + 4 < NC)
        def _():
            send_fields(c + 4)

        grid_chunk(c)

        @pl.when(c >= 4)
        def _():
            forward(c - 4)

        @pl.when(c + 5 < NC)
        def _():
            synthesise(c + 5)

        @pl.when(c == 4)
        def _():
            own_prev.wait()
            all_but_one(fp_r.at[pl.ds(0, NH - 1)], r0)
            for h in range(NH):
                for k in range(2):
                    first = (h % NX) * 64 + k * 32 + (h // NX) * 16
                    acc[first : first + 16, :] = fp_r[h, 16 * k : 16 * k + 16, :].astype(F32)

        @pl.when(c >= 5)
        def _():
            analyse(c - 5)

    forward(NC - 4)
    forward(NC - 3)
    analyse(NC - 5)
    forward(NC - 2)
    analyse(NC - 4)
    forward(NC - 1)
    analyse(NC - 3)
    analyse(NC - 2)
    forwarded(NC - 1)

    def result_copy(b, dest):
        return pltpu.make_async_remote_copy(
            src_ref=res_s.at[b, dest],
            dst_ref=out.at[:, mh, :, pl.ds(pl.multiple_of(b * LB, LB), LB)],
            send_sem=s4.at[b], recv_sem=r4.at[b],
            device_id=(dest, me), device_id_type=MESH,
        )

    def own_result(b):
        return pltpu.make_async_copy(
            res_s.at[b, mh], out.at[:, mh, :, pl.ds(pl.multiple_of(b * LB, LB), LB)], o4.at[b]
        )

    @pl.loop(0, NB)
    def _(b):
        lanes = pl.ds(pl.multiple_of(b * LB, LB), LB)
        total = acc[:, lanes] + analysed(NC - 1, b)
        rhs = jnp.concatenate(
            [
                jnp.concatenate(
                    [
                        total[(h % NX) * 64 + k * 32 + (h // NX) * 16 :][:16]
                        for h in range(NH)
                    ],
                    axis=0,
                )
                for k in range(2)
            ],
            axis=1,
        )
        high, low = split(rhs)
        mixed = jnp.dot(
            right_c[...], jnp.concatenate([high, high, low], axis=0), preferred_element_type=F32
        )
        damp = invden[:, lanes]
        high, low = split(mixed * jnp.concatenate([damp, damp], axis=1))
        res = jnp.dot(
            left_c[...], jnp.concatenate([high, high, low], axis=0), preferred_element_type=F32
        ).astype(BF)
        for k in range(2):
            res_s[b, :, k] = res[:, k * LB : k * LB + LB].reshape(NH, RL, LB)

        @pl.loop(1, NH)
        def _(i):
            result_copy(b, (mh + i) % NH).start()

        own_result(b).start()

    all_but_one(fp_s.at[pl.ds(0, NH - 1)], s0)

    @pl.loop(0, NC)
    def _(c):
        all_but_one(sbuf.at[c, :, pl.ds(0, NO - 1)], s1.at[c])
        all_but_one(spec_r.at[c, pl.ds(0, NP - 1)], s2.at[c])
        all_but_one(fwd_s.at[c, pl.ds(0, NX - 1)], s3.at[c])

    @pl.loop(0, NB)
    def _(b):
        all_but_one(res_s.at[b, pl.ds(0, NH - 1)], s4.at[b])
        own_result(b).wait()
        all_but_one(res_s.at[b, pl.ds(0, NH - 1)], r4.at[b])


def body(
    velocity, magnetic, legendre, quad_weight, order_table, field_prev, rates, radial_right, radial_left
):
    hbm = pl.BlockSpec(memory_space=pl.ANY)
    vmem = pl.BlockSpec(memory_space=pltpu.VMEM)
    sem = pltpu.SemaphoreType.DMA
    result = pl.pallas_call(
        kernel,
        out_shape=jax.ShapeDtypeStruct((2, SL, RL, NDEG), BF),
        in_specs=[hbm, hbm, hbm, vmem, vmem, hbm, vmem, vmem, vmem],
        out_specs=hbm,
        scratch_shapes=[
            pltpu.VMEM((4, SL, RL, NDEG), BF),
            pltpu.VMEM((4, SL, RL, NDEG), BF),
            pltpu.VMEM((NC, SL, NDEG, TC), BF),
            pltpu.VMEM((2, SL, RL, NDEG), F32),
            pltpu.VMEM((NH, 32, NDEG), BF),
            pltpu.VMEM((NH, 32, NDEG), BF),
            pltpu.VMEM((4, KK, TC), BF),
            pltpu.VMEM((KK, KK), BF),
            pltpu.VMEM((512, 512), BF),
            pltpu.VMEM((NLON, KK), BF),
            pltpu.VMEM((KK, NLON), BF),
            pltpu.VMEM((NC, 4, NO, 16, TC), BF),
            pltpu.VMEM((NC, 4, NO, 16, TC), BF),
            pltpu.VMEM((NLON, TC), BF),
            pltpu.VMEM((NC, NO, 2, 16, 128), BF),
            pltpu.VMEM((NC, NP, 16, 128), BF),
            pltpu.VMEM((NC, NX, 64, TC), BF),
            pltpu.VMEM((NC, NX, 64, TC), BF),
            pltpu.VMEM((256, NDEG), F32),
            pltpu.VMEM((NB, NH, 2, RL, LB), BF),
            pltpu.VMEM((128, NDEG), F32),
            pltpu.VMEM((128, 384), BF),
            pltpu.VMEM((128, 384), BF),
            sem((2,)),
            sem((NC, SL)),
            sem,
            sem, sem, sem,
            sem((NC,)), sem((NC,)), sem((NC,)),
            sem((NC,)), sem((NC,)), sem((NC,)),
            sem((NC,)), sem((NC,)), sem((NC,)),
            sem((NB,)), sem((NB,)), sem((NB,)),
        ],
        compiler_params=pltpu.CompilerParams(
            collective_id=0, has_side_effects=True, vmem_limit_bytes=58 * 1024 * 1024
        ),
        cost_estimate=pl.CostEstimate(
            flops=18_000_000_000, bytes_accessed=32_000_000, transcendentals=0
        ),
    )(
        velocity.reshape(4, SL, RL, NDEG),
        magnetic.reshape(4, SL, RL, NDEG),
        legendre,
        quad_weight.reshape(NLAT // 128, 128),
        order_table.reshape(1, 128),
        field_prev,
        rates.reshape(1, 128),
        radial_right,
        radial_left,
    )
    return result.astype(F32)


def solution(mesh):
    return jax.shard_map(
        body,
        mesh=mesh,
        in_specs=(
            P(None, None, "order", "shell", None),
            P(None, None, "order", "shell", None),
            P("order", None, None),
            P(),
            P(),
            P(None, "order", "shell", None),
            P(),
            P(),
            P(),
        ),
        out_specs=P(None, "order", "shell", None),
        check_vma=False,
    )
```
